32 devices in a mesh: groups: 2 (over x), row: 16 (over z, y, core).
Axes of the slice: x: 2, y: 2, z: 4, core: 2. Of those that a mesh axis runs over, the one named last changes fastest.
Arguments:
- hamiltonian: bfloat16 [96, 16, 128, 128], P(('groups', 'row')), parts along dimension 0, may hold values from -0.0625 to 0.0625
- coupling_cols: int32 [96, 16], P(('groups', 'row')), parts along dimension 0, may hold values from 0 to 47, as said below
- pattern_cols: int32 [96, 16], P(('groups', 'row')), parts along dimension 0, may hold values from 0 to 47, as said below
- current_term: bfloat16 [96, 16, 128, 128], P(('groups', 'row')), parts along dimension 0, may hold values from -6 to 6
- previous_term: bfloat16 [96, 16, 128, 128], P(('groups', 'row')), parts along dimension 0, may hold values from -6 to 6
Outputs:
- next_term: bfloat16 [96, 16, 128, 128], P(('groups', 'row')), parts along dimension 0
- after_term: bfloat16 [96, 16, 128, 128], P(('groups', 'row')), parts along dimension 0
The draws below stay inside these ranges and needn't reach their ends.
There are 2 independent parts, one for each index of `groups`. The reference program is written for one: setup_inputs(seed, part) draws one part's arguments, and reference() takes and returns one part's arrays. A program takes and returns all parts, laid end to end along the dimension named above; each array names one. Nothing has to cross between parts.
Inputs may be any that keep to these rules, and one draw needn't show every extreme that they name: `coupling_cols`: block row i holds 16 distinct block columns (i + o) mod 48, o from -8 to 8 in increasing order, i itself always among them. `pattern_cols`: block row i holds 16 distinct block columns (i + o) mod 48, o from -8 to 8 in increasing order, i itself always among them.
All inputs are finite; a program needn't handle non-finite values.
Results may differ from the reference program's by a relative error of at most 0.004.
Values may be sent and summed in bfloat16 or wider, within the bound.
A program may use at most 128 MiB of HBM per device.

```python
import jax
import jax.numpy as jnp
from jax import lax

BS = 128
REACH = 8
NNZ = 16
PNZ = 16
NB = 48


def band_pattern(key, width, reach):
    block_rows = jnp.arange(NB, dtype=jnp.int32)[:, None]
    dropped = jax.random.randint(key, (NB, 1), 0, 2 * reach, dtype=jnp.int32)
    dropped = dropped + (dropped >= reach).astype(jnp.int32)
    slots = jnp.arange(width, dtype=jnp.int32)[None, :]
    offsets = slots - reach + (slots >= dropped).astype(jnp.int32)
    return ((block_rows + offsets) % NB).astype(jnp.int32)


def draw_coupling_cols(key, part):
    key = jax.random.fold_in(key, 11)
    return band_pattern(key, NNZ, REACH)


def draw_pattern_cols(key, part):
    key = jax.random.fold_in(key, 23)
    return band_pattern(key, PNZ, REACH)


def steps_of(stream_key, dims, split, least, high):
    def one(dim, parts):
        heights = jax.random.uniform(jax.random.fold_in(jax.random.fold_in(stream_key, 6), dim), (parts,), jnp.float32, least / len(split), high / len(split))
        return jnp.repeat(jnp.exp(heights), dims[dim] // parts).reshape((-1,) + (1,) * (len(dims) - dim - 1))

    gain = one(*split[0])
    for cut in split[1:]:
        gain = gain * one(*cut)
    return gain


def centred(stream_key, extent, scale, most, pieces=(), kind=jnp.bfloat16):
    level = steps_of(stream_key, extent, pieces, -0.22, 0.18) if pieces else 1.0
    drawn = jax.random.normal(stream_key, extent, jnp.float32) * scale * level
    return jnp.minimum(jnp.maximum(drawn, -most), most).astype(kind)


def setup_inputs(seed: int = 0, part: int = 0) -> dict:
    splits = jax.random.split(jax.random.key(seed), 6)
    part_splits = jax.random.split(jax.random.fold_in(splits[5], part), 6)
    return {
        "hamiltonian": centred(part_splits[0], (NB, NNZ, BS, BS), (4 * NNZ * BS) ** -0.5, 0.0625, ((0, 16),)),
        "coupling_cols": draw_coupling_cols(jax.random.fold_in(jax.random.fold_in(splits[5], part), 71), part),
        "pattern_cols": draw_pattern_cols(jax.random.fold_in(jax.random.fold_in(splits[5], part), 71), part),
        "current_term": centred(part_splits[3], (NB, PNZ, BS, BS), 1.0, 6.0, ((0, 16),)),
        "previous_term": centred(part_splits[4], (NB, PNZ, BS, BS), 1.0, 6.0, ((0, 16),)),
    }


def advance(hamiltonian, coupling_cols, pattern_cols, current_term, previous_term):
    def advance_row(inputs):
        blocks, neighbours, own_cols, earlier = inputs
        picked = jnp.take(current_term, neighbours, axis=0).astype(jnp.float32)
        picked_cols = jnp.take(pattern_cols, neighbours, axis=0)
        matches = (own_cols[None, :, None] == picked_cols[:, None, :]).astype(jnp.float32)
        chosen = jnp.einsum("kmn,knab->kmab", matches, picked)
        product = jnp.einsum("kac,kmcb->mab", blocks.astype(jnp.float32), chosen)
        return (2.0 * product - earlier.astype(jnp.float32)).astype(jnp.bfloat16)

    return lax.map(advance_row, (hamiltonian, coupling_cols, pattern_cols, previous_term))


def reference(hamiltonian, coupling_cols, pattern_cols, current_term, previous_term):
    next_term = advance(hamiltonian, coupling_cols, pattern_cols, current_term, previous_term)
    after_term = advance(hamiltonian, coupling_cols, pattern_cols, next_term, current_term)
    return next_term, after_term
```

```python
import functools

import jax
import jax.numpy as jnp
from jax import lax
from jax.experimental import pallas as pl
from jax.experimental.pallas import tpu as pltpu
from jax.sharding import PartitionSpec as P

REACH = 8
BAND = 2 * REACH + 1


def exchanges(rows):
    window = rows + 2 * REACH
    plan = []
    for away in range(1, (REACH + rows - 1) // rows + 1):
        shift = away * rows
        for j in range(rows):
            distance = shift - j
            if distance <= REACH:
                plan.append((away, j, REACH + j - shift, shift, 0, BAND - distance))
            distance = shift + j - (rows - 1)
            if distance <= REACH:
                plan.append((-away, j, REACH + j + shift, j, j + shift, window - shift - j))
    return plan


def kernel(count, h_ref, coup_ref, patt_ref, cur_ref, prev_ref, next_ref, after_ref,
           hd, acc, win1, win2, send_sem, recv_sem):
    rows, slots, bs, _ = cur_ref.shape
    order = rows * count
    window = rows + 2 * REACH
    padded = window + window % 2
    plan = exchanges(rows)
    me = lax.axis_index("row")
    peers = sorted({entry[0] for entry in plan})

    def device(away):
        return {"row": lax.rem(me + (away + count), count)}

    barrier = pltpu.get_barrier_semaphore()
    for away in peers:
        pl.semaphore_signal(barrier, inc=1, device_id=device(away),
                            device_id_type=pl.DeviceIdType.MESH)

    def gap(ref, j):
        first = me * rows + (j - REACH - order)
        kept = jnp.int32(0)
        for m in range(slots):
            place = lax.rem(ref[j, m] - first, order)
            kept = kept + jnp.where(place == m, 1, 0).astype(jnp.int32)
        return kept

    def cols(c, n=1):
        return pl.ds(pl.multiple_of(c * bs, bs), n * bs)

    def spread(ref, j, o, d):
        same = jnp.where(o < d, 1.0, 0.0)
        past = jnp.where(o > d, 1.0, 0.0)
        return (ref[j, jnp.minimum(o, slots - 1)].astype(jnp.float32) * same
                + ref[j, jnp.maximum(o - 1, 0)].astype(jnp.float32) * past)

    def packed(ref, lead, j, m, d):
        same = jnp.where(m < d, 1.0, 0.0)
        return (ref[(*lead, cols(j + m))].astype(jnp.float32) * same
                + ref[(*lead, cols(j + m + 1))].astype(jnp.float32) * (1.0 - same))

    patt_gap = [gap(patt_ref, j) for j in range(rows)]
    coup_gap = [gap(coup_ref, j) for j in range(rows)]

    def copies(win, step, j):
        made = []
        for at, (away, row, there, first, land, width) in enumerate(plan):
            if row == j:
                made.append(pltpu.make_async_remote_copy(
                    src_ref=win.at[REACH + row, :, pl.ds(first * bs, width * bs)],
                    dst_ref=win.at[there, :, pl.ds(land * bs, width * bs)],
                    send_sem=send_sem.at[step, at],
                    recv_sem=recv_sem.at[step, at],
                    device_id=device(away),
                    device_id_type=pl.DeviceIdType.MESH,
                ))
        return made

    first_copies = []
    for j in range(rows):
        d = patt_gap[j]

        @pl.loop(0, BAND)
        def _(o):
            win1[REACH + j, :, cols(j + o)] = spread(cur_ref, j, o, d).astype(jnp.bfloat16)

        if j == 0:
            pl.semaphore_wait(barrier, len(peers))
        for copy in copies(win1, 0, j):
            copy.start()
            first_copies.append(copy)

    hd[...] = jnp.zeros_like(hd)
    for j in range(rows):
        d = coup_gap[j]

        @pl.loop(0, BAND)
        def _(o):
            hd[j * bs:(j + 1) * bs, cols(j + o)] = spread(h_ref, j, o, d).astype(jnp.bfloat16)

    for win in (win1, win2):
        for l in range(window):
            if l > REACH:
                n = l - REACH
                win[l, :, 0:n * bs] = jnp.zeros((bs, n * bs), jnp.bfloat16)
            if l + REACH + 1 < padded:
                n = padded - (l + REACH + 1)
                win[l, :, (l + REACH + 1) * bs:] = jnp.zeros((bs, n * bs), jnp.bfloat16)

    def multiply(win):
        @pl.loop(0, padded // 2)
        def _(t):
            right = win[:, :, cols(2 * t, 2)].reshape(window * bs, 2 * bs)
            acc[:, cols(2 * t, 2)] = jnp.dot(hd[...], right, preferred_element_type=jnp.float32)

    for copy in first_copies:
        copy.wait_recv()
    multiply(win1)

    second_copies = []
    for j in range(rows):
        d = patt_gap[j]

        @pl.loop(0, BAND)
        def _(o):
            keep = jnp.where(o == d, 0.0, 1.0)
            block = 2.0 * acc[j * bs:(j + 1) * bs, cols(j + o)] - spread(prev_ref, j, o, d)
            win2[REACH + j, :, cols(j + o)] = (block * keep).astype(jnp.bfloat16)

        for copy in copies(win2, 1, j):
            copy.start()
            second_copies.append(copy)

    for j in range(rows):
        d = patt_gap[j]

        @pl.loop(0, slots)
        def _(m):
            next_ref[j, m] = packed(win2, (REACH + j, slice(None)), j, m, d).astype(jnp.bfloat16)

    for copy in second_copies:
        copy.wait_recv()
    multiply(win2)

    for j in range(rows):
        d = patt_gap[j]

        @pl.loop(0, slots)
        def _(m):
            total = packed(acc, (slice(j * bs, (j + 1) * bs),), j, m, d)
            block = 2.0 * total - cur_ref[j, m].astype(jnp.float32)
            after_ref[j, m] = block.astype(jnp.bfloat16)

    for copy in first_copies + second_copies:
        copy.wait_send()


def body(count, hamiltonian, coupling_cols, pattern_cols, current_term, previous_term):
    rows, slots, bs, _ = current_term.shape
    window = rows + 2 * REACH
    padded = window + window % 2
    made = len(exchanges(rows))
    vmem = pl.BlockSpec(memory_space=pltpu.VMEM)
    smem = pl.BlockSpec(memory_space=pltpu.SMEM)
    term = jax.ShapeDtypeStruct(current_term.shape, jnp.bfloat16)
    return pl.pallas_call(
        functools.partial(kernel, count),
        out_shape=(term, term),
        in_specs=[vmem, smem, smem, vmem, vmem],
        out_specs=(vmem, vmem),
        scratch_shapes=[
            pltpu.VMEM((rows * bs, window * bs), jnp.bfloat16),
            pltpu.VMEM((rows * bs, padded * bs), jnp.float32),
            pltpu.VMEM((window, bs, padded * bs), jnp.bfloat16),
            pltpu.VMEM((window, bs, padded * bs), jnp.bfloat16),
            pltpu.SemaphoreType.DMA((2, made)),
            pltpu.SemaphoreType.DMA((2, made)),
        ],
        compiler_params=pltpu.CompilerParams(
            collective_id=0, has_side_effects=True, vmem_limit_bytes=52 * 2**20
        ),
    )(hamiltonian, coupling_cols, pattern_cols, current_term, previous_term)


def solution(mesh):
    split = P(("groups", "row"), None, None, None)
    placed = (split, P(("groups", "row"), None), P(("groups", "row"), None), split, split)
    return jax.shard_map(
        functools.partial(body, mesh.shape["row"]),
        mesh=mesh,
        in_specs=placed,
        out_specs=(split, split),
        check_vma=False,
    )
```

```python
import functools

import jax
import jax.numpy as jnp
from jax import lax
from jax.experimental import pallas as pl
from jax.experimental.pallas import tpu as pltpu
from jax.sharding import PartitionSpec as P

REACH = 8
BAND = 2 * REACH + 1


def exchanges(rows):
    window = rows + 2 * REACH
    plan = []
    for away in range(1, (REACH + rows - 1) // rows + 1):
        shift = away * rows
        for j in range(rows):
            distance = shift - j
            if distance <= REACH:
                plan.append((away, j, REACH + j - shift, shift, 0, BAND - distance))
            distance = shift + j - (rows - 1)
            if distance <= REACH:
                plan.append((-away, j, REACH + j + shift, j, j + shift, window - shift - j))
    return plan


def kernel(count, h_ref, coup_ref, patt_ref, cur_ref, prev_ref, next_ref, after_ref,
           hd, acc, win1, win2, send_sem, forward_sem, recv_sem):
    rows, slots, bs, _ = cur_ref.shape
    order = rows * count
    window = rows + 2 * REACH
    padded = window + window % 2
    plan = exchanges(rows)
    me = lax.axis_index("row")
    peers = sorted({entry[0] for entry in plan})

    def device(away):
        return {"row": lax.rem(me + (away + count), count)}

    barrier = pltpu.get_barrier_semaphore()
    for away in peers:
        pl.semaphore_signal(barrier, inc=1, device_id=device(away),
                            device_id_type=pl.DeviceIdType.MESH)

    def gap(ref, j):
        first = me * rows + (j - REACH - order)
        kept = jnp.int32(0)
        for m in range(slots):
            place = lax.rem(ref[j, m] - first, order)
            kept = kept + jnp.where(place == m, 1, 0).astype(jnp.int32)
        return kept

    def cols(c, n=1):
        return pl.ds(pl.multiple_of(c * bs, bs), n * bs)

    def spread(ref, j, o, d):
        same = jnp.where(o < d, 1.0, 0.0)
        past = jnp.where(o > d, 1.0, 0.0)
        return (ref[j, jnp.minimum(o, slots - 1)].astype(jnp.float32) * same
                + ref[j, jnp.maximum(o - 1, 0)].astype(jnp.float32) * past)

    def packed(ref, lead, j, m, d):
        same = jnp.where(m < d, 1.0, 0.0)
        return (ref[(*lead, cols(j + m))].astype(jnp.float32) * same
                + ref[(*lead, cols(j + m + 1))].astype(jnp.float32) * (1.0 - same))

    patt_gap = [gap(patt_ref, j) for j in range(rows)]
    coup_gap = [gap(coup_ref, j) for j in range(rows)]

    even = lax.rem(me, 2) == 0
    direct = {0: (2, -1, -3, 1), 1: (-2, 1, 3, -1)}
    handed = {0: {1: 2, 2: 3}, 1: {-1: -2, -2: -3}}
    at_of = {entry[:2]: at for at, entry in enumerate(plan)}

    def remote(win, step, src, at, sent, away):
        _, _, there, _, land, width = plan[at]
        return pltpu.make_async_remote_copy(
            src_ref=win.at[src[0], :, pl.ds(src[1] * bs, width * bs)],
            dst_ref=win.at[there, :, pl.ds(land * bs, width * bs)],
            send_sem=sent.at[step, at],
            recv_sem=recv_sem.at[step, at],
            device_id=device(away),
            device_id_type=pl.DeviceIdType.MESH,
        )

    def own(win, step, core, j):
        keys = [(away, j) for away in direct[core] if (away, j) in at_of]
        return [remote(win, step, (REACH + j, plan[at_of[key]][3]), at_of[key], send_sem, key[0])
                for key in keys]

    def passed(win, step, core):
        side = 1 if core == 0 else -1
        made = []
        for j in range(rows):
            for away, onward in handed[core].items():
                if (onward, j) in at_of:
                    at = at_of[onward, j]
                    src = (plan[at][2] + side * rows, plan[at][4] + side * rows)
                    made.append((at_of[away, j], remote(win, step, src, at, forward_sem, side)))
        return made

    def arrival(win, step, at):
        return remote(win, step, (REACH, 0), at, send_sem, plan[at][0])

    def on_core(core):
        return pl.when(even if core == 0 else jnp.logical_not(even))

    def start_rows(win, step, j):
        for core in (0, 1):
            @on_core(core)
            def _(core=core):
                for copy in own(win, step, core, j):
                    copy.start()

    def receive(win, step):
        for core in (0, 1):
            @on_core(core)
            def _(core=core):
                done = set()
                for at, copy in passed(win, step, core):
                    arrival(win, step, at).wait_recv()
                    copy.start()
                    done.add(at)
                for at in range(len(plan)):
                    if at not in done:
                        arrival(win, step, at).wait_recv()

    def finish(win, step):
        for core in (0, 1):
            @on_core(core)
            def _(core=core):
                for j in range(rows):
                    for copy in own(win, step, core, j):
                        copy.wait_send()
                for _, copy in passed(win, step, core):
                    copy.wait_send()

    for j in range(rows):
        d = patt_gap[j]

        @pl.loop(0, BAND)
        def _(o):
            win1[REACH + j, :, cols(j + o)] = spread(cur_ref, j, o, d).astype(jnp.bfloat16)

        if j == 0:
            pl.semaphore_wait(barrier, len(peers))
        start_rows(win1, 0, j)

    hd[...] = jnp.zeros_like(hd)
    for j in range(rows):
        d = coup_gap[j]

        @pl.loop(0, BAND)
        def _(o):
            hd[j * bs:(j + 1) * bs, cols(j + o)] = spread(h_ref, j, o, d).astype(jnp.bfloat16)

    for win in (win1, win2):
        for l in range(window):
            if l > REACH:
                n = l - REACH
                win[l, :, 0:n * bs] = jnp.zeros((bs, n * bs), jnp.bfloat16)
            if l + REACH + 1 < padded:
                n = padded - (l + REACH + 1)
                win[l, :, (l + REACH + 1) * bs:] = jnp.zeros((bs, n * bs), jnp.bfloat16)

    def multiply(win):
        @pl.loop(0, padded // 2)
        def _(t):
            right = win[:, :, cols(2 * t, 2)].reshape(window * bs, 2 * bs)
            acc[:, cols(2 * t, 2)] = jnp.dot(hd[...], right, preferred_element_type=jnp.float32)

    receive(win1, 0)
    multiply(win1)

    for j in range(rows):
        d = patt_gap[j]

        @pl.loop(0, BAND)
        def _(o):
            keep = jnp.where(o == d, 0.0, 1.0)
            block = 2.0 * acc[j * bs:(j + 1) * bs, cols(j + o)] - spread(prev_ref, j, o, d)
            win2[REACH + j, :, cols(j + o)] = (block * keep).astype(jnp.bfloat16)

        start_rows(win2, 1, j)

    for j in range(rows):
        d = patt_gap[j]

        @pl.loop(0, slots)
        def _(m):
            next_ref[j, m] = packed(win2, (REACH + j, slice(None)), j, m, d).astype(jnp.bfloat16)

    receive(win2, 1)
    multiply(win2)

    for j in range(rows):
        d = patt_gap[j]

        @pl.loop(0, slots)
        def _(m):
            total = packed(acc, (slice(j * bs, (j + 1) * bs),), j, m, d)
            block = 2.0 * total - cur_ref[j, m].astype(jnp.float32)
            after_ref[j, m] = block.astype(jnp.bfloat16)

    finish(win1, 0)
    finish(win2, 1)


def body(count, hamiltonian, coupling_cols, pattern_cols, current_term, previous_term):
    rows, slots, bs, _ = current_term.shape
    window = rows + 2 * REACH
    padded = window + window % 2
    made = len(exchanges(rows))
    vmem = pl.BlockSpec(memory_space=pltpu.VMEM)
    smem = pl.BlockSpec(memory_space=pltpu.SMEM)
    term = jax.ShapeDtypeStruct(current_term.shape, jnp.bfloat16)
    return pl.pallas_call(
        functools.partial(kernel, count),
        out_shape=(term, term),
        in_specs=[vmem, smem, smem, vmem, vmem],
        out_specs=(vmem, vmem),
        scratch_shapes=[
            pltpu.VMEM((rows * bs, window * bs), jnp.bfloat16),
            pltpu.VMEM((rows * bs, padded * bs), jnp.float32),
            pltpu.VMEM((window, bs, padded * bs), jnp.bfloat16),
            pltpu.VMEM((window, bs, padded * bs), jnp.bfloat16),
            pltpu.SemaphoreType.DMA((2, made)),
            pltpu.SemaphoreType.DMA((2, made)),
            pltpu.SemaphoreType.DMA((2, made)),
        ],
        compiler_params=pltpu.CompilerParams(
            collective_id=0, has_side_effects=True, vmem_limit_bytes=52 * 2**20
        ),
    )(hamiltonian, coupling_cols, pattern_cols, current_term, previous_term)


def solution(mesh):
    split = P(("groups", "row"), None, None, None)
    placed = (split, P(("groups", "row"), None), P(("groups", "row"), None), split, split)
    return jax.shard_map(
        functools.partial(body, mesh.shape["row"]),
        mesh=mesh,
        in_specs=placed,
        out_specs=(split, split),
        check_vma=False,
    )
```

```python
import functools

import jax
import jax.numpy as jnp
from jax import lax
from jax.experimental import pallas as pl
from jax.experimental.pallas import tpu as pltpu
from jax.sharding import PartitionSpec as P

REACH = 8
BAND = 2 * REACH + 1


def exchanges(rows):
    window = rows + 2 * REACH
    plan = []
    for away in range(1, (REACH + rows - 1) // rows + 1):
        shift = away * rows
        for j in range(rows):
            distance = shift - j
            if distance <= REACH:
                plan.append((away, j, REACH + j - shift, shift, 0, BAND - distance))
            distance = shift + j - (rows - 1)
            if distance <= REACH:
                plan.append((-away, j, REACH + j + shift, j, j + shift, window - shift - j))
    return plan


def kernel(count, h_ref, coup_ref, patt_ref, cur_ref, prev_ref, next_ref, after_ref,
           hd, acc, win1, win2, send_sem, forward_sem, relay_sem, recv_sem):
    rows, slots, bs, _ = cur_ref.shape
    order = rows * count
    window = rows + 2 * REACH
    padded = window + window % 2
    plan = exchanges(rows)
    me = lax.axis_index("row")
    peers = sorted({entry[0] for entry in plan})

    def device(away):
        return {"row": lax.rem(me + (away + count), count)}

    barrier = pltpu.get_barrier_semaphore()
    for away in peers:
        pl.semaphore_signal(barrier, inc=1, device_id=device(away),
                            device_id_type=pl.DeviceIdType.MESH)

    def gap(ref, j):
        first = me * rows + (j - REACH - order)
        kept = jnp.int32(0)
        for m in range(slots):
            place = lax.rem(ref[j, m] - first, order)
            kept = kept + jnp.where(place == m, 1, 0).astype(jnp.int32)
        return kept

    def cols(c, n=1):
        return pl.ds(pl.multiple_of(c * bs, bs), n * bs)

    def spread(ref, j, o, d):
        same = jnp.where(o < d, 1.0, 0.0)
        past = jnp.where(o > d, 1.0, 0.0)
        return (ref[j, jnp.minimum(o, slots - 1)].astype(jnp.float32) * same
                + ref[j, jnp.maximum(o - 1, 0)].astype(jnp.float32) * past)

    def packed(ref, lead, j, m, d):
        same = jnp.where(m < d, 1.0, 0.0)
        return (ref[(*lead, cols(j + m))].astype(jnp.float32) * same
                + ref[(*lead, cols(j + m + 1))].astype(jnp.float32) * (1.0 - same))

    patt_gap = [gap(patt_ref, j) for j in range(rows)]
    coup_gap = [gap(coup_ref, j) for j in range(rows)]

    role = lax.rem(me, 4)
    direct = {0: (2, -1, -3, 1), 1: (1, -2, 3, -1), 2: (-1, 2, -3, 1), 3: (-2, 1, 3, -1)}
    handed = {0: {1: 2, 2: 3}, 1: {-1: -2, -2: -3}}
    relayed = {0: {}, 1: {-1: 2, -2: 1}, 2: {1: -2, 2: -1}, 3: {}}
    at_of = {entry[:2]: at for at, entry in enumerate(plan)}
    shared = BAND - 1 - 2 * rows

    def parts(at, core):
        away, width = plan[at][0], plan[at][5]
        if core == 0 and away in (1, 2):
            return ((0, shared), (shared, width - shared))
        if core == 1 and away in (-1, -2):
            return ((width - shared, shared), (0, width - shared))
        return ((0, width),)

    def remote(win, step, at, part, core, row, shift, sent, away):
        _, _, there, _, land, _ = plan[at]
        first, width = parts(at, core)[part]
        first = first + land
        return pltpu.make_async_remote_copy(
            src_ref=win.at[row, :, pl.ds((first + shift) * bs, width * bs)],
            dst_ref=win.at[there, :, pl.ds(first * bs, width * bs)],
            send_sem=sent.at[step, at, part],
            recv_sem=recv_sem.at[step, at, part],
            device_id=device(away),
            device_id_type=pl.DeviceIdType.MESH,
        )

    def own(win, step, part_role, j):
        made = []
        for away in direct[part_role]:
            if (away, j) in at_of:
                at = at_of[away, j]
                core = (part_role + away) % 2
                split = len(parts(at, core)) == 2
                for part in range(2 if split else 1):
                    if split and part == 0 and (away > 0) == (part_role >= 2):
                        continue
                    made.append(remote(win, step, at, part, core, REACH + j, away * rows,
                                       send_sem, away))
        return made

    def onward(win, step, at, part, core, side, sent):
        return remote(win, step, at, part, core, plan[at][2] + side * rows, side * rows, sent, side)

    def arrival(win, step, at, part, core):
        first = plan[at][4] + parts(at, core)[part][0]
        return remote(win, step, at, part, core, REACH, -first, send_sem, plan[at][0])

    def receive(win, step, part_role):
        core = part_role % 2
        made = []
        done = set()
        for j in range(rows):
            for away, further in handed[core].items():
                at = at_of[away, j]
                done.add(at)
                arrival(win, step, at, 0, core).wait_recv()
                if away in relayed[part_role]:
                    copy = onward(win, step, at_of[relayed[part_role][away], j], 0, 1 - core,
                                  3 if core else -3, relay_sem)
                    copy.start()
                    made.append(copy)
                arrival(win, step, at, 1, core).wait_recv()
                if (further, j) in at_of:
                    copy = onward(win, step, at_of[further, j], 0, 1 - core,
                                  -1 if core else 1, forward_sem)
                    copy.start()
                    made.append(copy)
        for at in range(len(plan)):
            if at not in done:
                arrival(win, step, at, 0, core).wait_recv()
        return made

    def by_role(act):
        for part_role in range(4):
            @pl.when(role == part_role)
            def _(part_role=part_role):
                act(part_role)

    def start_rows(win, step, j):
        def act(part_role):
            for copy in own(win, step, part_role, j):
                copy.start()

        by_role(act)

    def receive_all(win, step):
        def act(part_role):
            for copy in receive(win, step, part_role):
                copy.wait_send()
            for j in range(rows):
                for copy in own(win, step, part_role, j):
                    copy.wait_send()

        by_role(act)

    for j in range(rows):
        d = patt_gap[j]

        @pl.loop(0, BAND)
        def _(o):
            win1[REACH + j, :, cols(j + o)] = spread(cur_ref, j, o, d).astype(jnp.bfloat16)

        if j == 0:
            pl.semaphore_wait(barrier, len(peers))
        start_rows(win1, 0, j)

    hd[...] = jnp.zeros_like(hd)
    for j in range(rows):
        d = coup_gap[j]

        @pl.loop(0, BAND)
        def _(o):
            hd[j * bs:(j + 1) * bs, cols(j + o)] = spread(h_ref, j, o, d).astype(jnp.bfloat16)

    for win in (win1, win2):
        for l in range(window):
            if l > REACH:
                n = l - REACH
                win[l, :, 0:n * bs] = jnp.zeros((bs, n * bs), jnp.bfloat16)
            if l + REACH + 1 < padded:
                n = padded - (l + REACH + 1)
                win[l, :, (l + REACH + 1) * bs:] = jnp.zeros((bs, n * bs), jnp.bfloat16)

    def multiply(win):
        @pl.loop(0, padded // 2)
        def _(t):
            right = win[:, :, cols(2 * t, 2)].reshape(window * bs, 2 * bs)
            acc[:, cols(2 * t, 2)] = jnp.dot(hd[...], right, preferred_element_type=jnp.float32)

    receive_all(win1, 0)
    multiply(win1)

    for j in range(rows):
        d = patt_gap[j]

        @pl.loop(0, BAND)
        def _(o):
            keep = jnp.where(o == d, 0.0, 1.0)
            block = 2.0 * acc[j * bs:(j + 1) * bs, cols(j + o)] - spread(prev_ref, j, o, d)
            win2[REACH + j, :, cols(j + o)] = (block * keep).astype(jnp.bfloat16)

        start_rows(win2, 1, j)

    for j in range(rows):
        d = patt_gap[j]

        @pl.loop(0, slots)
        def _(m):
            next_ref[j, m] = packed(win2, (REACH + j, slice(None)), j, m, d).astype(jnp.bfloat16)

    receive_all(win2, 1)
    multiply(win2)

    for j in range(rows):
        d = patt_gap[j]

        @pl.loop(0, slots)
        def _(m):
            total = packed(acc, (slice(j * bs, (j + 1) * bs),), j, m, d)
            block = 2.0 * total - cur_ref[j, m].astype(jnp.float32)
            after_ref[j, m] = block.astype(jnp.bfloat16)


def body(count, hamiltonian, coupling_cols, pattern_cols, current_term, previous_term):
    rows, slots, bs, _ = current_term.shape
    window = rows + 2 * REACH
    padded = window + window % 2
    made = len(exchanges(rows))
    vmem = pl.BlockSpec(memory_space=pltpu.VMEM)
    smem = pl.BlockSpec(memory_space=pltpu.SMEM)
    term = jax.ShapeDtypeStruct(current_term.shape, jnp.bfloat16)
    return pl.pallas_call(
        functools.partial(kernel, count),
        out_shape=(term, term),
        in_specs=[vmem, smem, smem, vmem, vmem],
        out_specs=(vmem, vmem),
        scratch_shapes=[
            pltpu.VMEM((rows * bs, window * bs), jnp.bfloat16),
            pltpu.VMEM((rows * bs, padded * bs), jnp.float32),
            pltpu.VMEM((window, bs, padded * bs), jnp.bfloat16),
            pltpu.VMEM((window, bs, padded * bs), jnp.bfloat16),
            pltpu.SemaphoreType.DMA((2, made, 2)),
            pltpu.SemaphoreType.DMA((2, made, 2)),
            pltpu.SemaphoreType.DMA((2, made, 2)),
            pltpu.SemaphoreType.DMA((2, made, 2)),
        ],
        compiler_params=pltpu.CompilerParams(
            collective_id=0, has_side_effects=True, vmem_limit_bytes=52 * 2**20
        ),
    )(hamiltonian, coupling_cols, pattern_cols, current_term, previous_term)


def solution(mesh):
    split = P(("groups", "row"), None, None, None)
    placed = (split, P(("groups", "row"), None), P(("groups", "row"), None), split, split)
    return jax.shard_map(
        functools.partial(body, mesh.shape["row"]),
        mesh=mesh,
        in_specs=placed,
        out_specs=(split, split),
        check_vma=False,
    )
```

```python
import functools

import jax
import jax.numpy as jnp
from jax import lax
from jax.experimental import pallas as pl
from jax.experimental.pallas import tpu as pltpu
from jax.sharding import PartitionSpec as P

REACH = 8
BAND = 2 * REACH + 1


def exchanges(rows):
    window = rows + 2 * REACH
    plan = []
    for away in range(1, (REACH + rows - 1) // rows + 1):
        shift = away * rows
        for j in range(rows):
            distance = shift - j
            if distance <= REACH:
                plan.append((away, j, REACH + j - shift, shift, 0, BAND - distance))
            distance = shift + j - (rows - 1)
            if distance <= REACH:
                plan.append((-away, j, REACH + j + shift, j, j + shift, window - shift - j))
    return plan


def kernel(count, h_ref, coup_ref, patt_ref, cur_ref, prev_ref, next_ref, after_ref,
           hd, acc, win1, win2, send_sem, forward_sem, relay_sem, recv_sem):
    rows, slots, bs, _ = cur_ref.shape
    order = rows * count
    window = rows + 2 * REACH
    padded = window + window % 2
    plan = exchanges(rows)
    me = lax.axis_index("row")
    peers = sorted({entry[0] for entry in plan})

    def device(away):
        return {"row": lax.rem(me + (away + count), count)}

    barrier = pltpu.get_barrier_semaphore()
    for away in peers:
        pl.semaphore_signal(barrier, inc=1, device_id=device(away),
                            device_id_type=pl.DeviceIdType.MESH)

    def gap(ref, j):
        first = me * rows + (j - REACH - order)
        kept = jnp.int32(0)
        for m in range(slots):
            place = lax.rem(ref[j, m] - first, order)
            kept = kept + jnp.where(place == m, 1, 0).astype(jnp.int32)
        return kept

    def cols(c, n=1):
        return pl.ds(pl.multiple_of(c * bs, bs), n * bs)

    def spread(ref, j, o, d):
        same = jnp.where(o < d, 1.0, 0.0)
        past = jnp.where(o > d, 1.0, 0.0)
        return (ref[j, jnp.minimum(o, slots - 1)].astype(jnp.float32) * same
                + ref[j, jnp.maximum(o - 1, 0)].astype(jnp.float32) * past)

    def packed(ref, lead, j, m, d):
        same = jnp.where(m < d, 1.0, 0.0)
        return (ref[(*lead, cols(j + m))].astype(jnp.float32) * same
                + ref[(*lead, cols(j + m + 1))].astype(jnp.float32) * (1.0 - same))

    patt_gap = [gap(patt_ref, j) for j in range(rows)]
    coup_gap = [gap(coup_ref, j) for j in range(rows)]

    role = lax.rem(me, 4)
    direct = {0: (2, -1, -3, 1), 1: (1, -2, 3, -1), 2: (-1, 2, -3, 1), 3: (-2, 1, 3, -1)}
    handed = {0: {1: 2, 2: 3}, 1: {-1: -2, -2: -3}}
    relayed = {0: {}, 1: {-1: 2, -2: 1}, 2: {1: -2, 2: -1}, 3: {}}
    at_of = {entry[:2]: at for at, entry in enumerate(plan)}
    shared = BAND - 1 - 2 * rows

    def parts(at, core):
        away, width = plan[at][0], plan[at][5]
        if core == 0 and away in (1, 2):
            return ((0, shared), (shared, width - shared))
        if core == 1 and away in (-1, -2):
            return ((width - shared, shared), (0, width - shared))
        return ((0, width),)

    def remote(win, step, at, part, core, row, shift, sent, away):
        _, _, there, _, land, _ = plan[at]
        first, width = parts(at, core)[part]
        first = first + land
        return pltpu.make_async_remote_copy(
            src_ref=win.at[row, :, pl.ds((first + shift) * bs, width * bs)],
            dst_ref=win.at[there, :, pl.ds(first * bs, width * bs)],
            send_sem=sent.at[step, at, part],
            recv_sem=recv_sem.at[step, at, part],
            device_id=device(away),
            device_id_type=pl.DeviceIdType.MESH,
        )

    def own(win, step, part_role, j):
        made = []
        for away in direct[part_role]:
            if (away, j) in at_of:
                at = at_of[away, j]
                core = (part_role + away) % 2
                split = len(parts(at, core)) == 2
                for part in range(2 if split else 1):
                    if split and part == 0 and (away > 0) == (part_role >= 2):
                        continue
                    made.append(remote(win, step, at, part, core, REACH + j, away * rows,
                                       send_sem, away))
        return made

    def onward(win, step, at, part, core, side, sent):
        return remote(win, step, at, part, core, plan[at][2] + side * rows, side * rows, sent, side)

    def arrival(win, step, at, part, core):
        first = plan[at][4] + parts(at, core)[part][0]
        return remote(win, step, at, part, core, REACH, -first, send_sem, plan[at][0])

    def receive(win, step, part_role):
        core = part_role % 2
        made = []
        done = set()
        for j in range(rows):
            for away, further in handed[core].items():
                at = at_of[away, j]
                done.add(at)
                arrival(win, step, at, 0, core).wait_recv()
                if away in relayed[part_role]:
                    copy = onward(win, step, at_of[relayed[part_role][away], j], 0, 1 - core,
                                  3 if core else -3, relay_sem)
                    copy.start()
                    made.append(copy)
                arrival(win, step, at, 1, core).wait_recv()
                if (further, j) in at_of:
                    copy = onward(win, step, at_of[further, j], 0, 1 - core,
                                  -1 if core else 1, forward_sem)
                    copy.start()
                    made.append(copy)
        for at in range(len(plan)):
            if at not in done:
                arrival(win, step, at, 0, core).wait_recv()
        return made

    def by_role(act):
        for part_role in range(4):
            @pl.when(role == part_role)
            def _(part_role=part_role):
                act(part_role)

    def start_rows(win, step, j):
        def act(part_role):
            for copy in own(win, step, part_role, j):
                copy.start()

        by_role(act)

    def receive_all(win, step):
        def act(part_role):
            for copy in receive(win, step, part_role):
                copy.wait_send()
            for j in range(rows):
                for copy in own(win, step, part_role, j):
                    copy.wait_send()

        by_role(act)

    for j in range(rows):
        d = patt_gap[j]

        @pl.loop(0, BAND)
        def _(o):
            win1[REACH + j, :, cols(j + o)] = spread(cur_ref, j, o, d).astype(jnp.bfloat16)

        if j == 0:
            pl.semaphore_wait(barrier, len(peers))
        start_rows(win1, 0, j)

    hd[...] = jnp.zeros_like(hd)
    for j in range(rows):
        d = coup_gap[j]

        @pl.loop(0, BAND)
        def _(o):
            hd[j * bs:(j + 1) * bs, cols(j + o)] = spread(h_ref, j, o, d).astype(jnp.bfloat16)

    for win in (win1, win2):
        for l in range(window):
            if l > REACH:
                n = l - REACH
                win[l, :, 0:n * bs] = jnp.zeros((bs, n * bs), jnp.bfloat16)
            if l + REACH + 1 < padded:
                n = padded - (l + REACH + 1)
                win[l, :, (l + REACH + 1) * bs:] = jnp.zeros((bs, n * bs), jnp.bfloat16)

    def multiply(win):
        for c in range(0, padded, 2):
            low, high = max(0, c - REACH), min(window, c + REACH + 2)
            right = win[low:high, :, c * bs:(c + 2) * bs].reshape((high - low) * bs, 2 * bs)
            left = hd[:, low * bs:high * bs]
            acc[:, c * bs:(c + 2) * bs] = jnp.dot(left, right, preferred_element_type=jnp.float32)

    receive_all(win1, 0)
    multiply(win1)

    for j in range(rows):
        d = patt_gap[j]

        @pl.loop(0, BAND)
        def _(o):
            keep = jnp.where(o == d, 0.0, 1.0)
            block = 2.0 * acc[j * bs:(j + 1) * bs, cols(j + o)] - spread(prev_ref, j, o, d)
            win2[REACH + j, :, cols(j + o)] = (block * keep).astype(jnp.bfloat16)

        start_rows(win2, 1, j)

    for j in range(rows):
        d = patt_gap[j]

        @pl.loop(0, slots)
        def _(m):
            next_ref[j, m] = packed(win2, (REACH + j, slice(None)), j, m, d).astype(jnp.bfloat16)

    receive_all(win2, 1)
    multiply(win2)

    for j in range(rows):
        d = patt_gap[j]

        @pl.loop(0, slots)
        def _(m):
            total = packed(acc, (slice(j * bs, (j + 1) * bs),), j, m, d)
            block = 2.0 * total - cur_ref[j, m].astype(jnp.float32)
            after_ref[j, m] = block.astype(jnp.bfloat16)


def body(count, hamiltonian, coupling_cols, pattern_cols, current_term, previous_term):
    rows, slots, bs, _ = current_term.shape
    window = rows + 2 * REACH
    padded = window + window % 2
    made = len(exchanges(rows))
    vmem = pl.BlockSpec(memory_space=pltpu.VMEM)
    smem = pl.BlockSpec(memory_space=pltpu.SMEM)
    term = jax.ShapeDtypeStruct(current_term.shape, jnp.bfloat16)
    return pl.pallas_call(
        functools.partial(kernel, count),
        out_shape=(term, term),
        in_specs=[vmem, smem, smem, vmem, vmem],
        out_specs=(vmem, vmem),
        scratch_shapes=[
            pltpu.VMEM((rows * bs, window * bs), jnp.bfloat16),
            pltpu.VMEM((rows * bs, padded * bs), jnp.float32),
            pltpu.VMEM((window, bs, padded * bs), jnp.bfloat16),
            pltpu.VMEM((window, bs, padded * bs), jnp.bfloat16),
            pltpu.SemaphoreType.DMA((2, made, 2)),
            pltpu.SemaphoreType.DMA((2, made, 2)),
            pltpu.SemaphoreType.DMA((2, made, 2)),
            pltpu.SemaphoreType.DMA((2, made, 2)),
        ],
        compiler_params=pltpu.CompilerParams(
            collective_id=0, has_side_effects=True, vmem_limit_bytes=52 * 2**20
        ),
    )(hamiltonian, coupling_cols, pattern_cols, current_term, previous_term)


def solution(mesh):
    split = P(("groups", "row"), None, None, None)
    placed = (split, P(("groups", "row"), None), P(("groups", "row"), None), split, split)
    return jax.shard_map(
        functools.partial(body, mesh.shape["row"]),
        mesh=mesh,
        in_specs=placed,
        out_specs=(split, split),
        check_vma=False,
    )
```
